256 devices in a mesh: rows: 32 (over z, x), cols: 8 (over y, core).
Axes of the slice: x: 4, y: 4, z: 8, core: 2. Of those that a mesh axis runs over, the one named last changes fastest.
Arguments:
- features: bfloat16 [256, 131072], P('cols', 'rows'), may hold values from -6 to 6
- weight: bfloat16 [256, 256], replicated, may hold values from -0.375 to 0.375
- adj_tiles: bfloat16 [32768, 128, 128], P('rows'), may hold values from -0.09375 to 0.09375
- tile_rows: int32 [32768], P('rows'), may hold values from 0 to 31
- tile_cols: int32 [32768], P('rows'), may hold values from 0 to 1023
- tile_count: int32 [32], P('rows'), may hold values from 512 to 1024, as said below
- cotangent: bfloat16 [256, 131072], P('cols', 'rows'), may hold values from -6 to 6
Outputs:
- aggregated: bfloat16 [256, 131072], P('cols', 'rows')
- grad_features: bfloat16 [256, 131072], P('cols', 'rows')
- grad_weight: float32 [256, 256], replicated
The draws below stay inside these ranges and needn't reach their ends.
Inputs may be any that keep to these rules, and one draw needn't show every extreme that they name: `tile_count`: some index of rows uses all 1024 slots in every draw.
All inputs are finite; a program needn't handle non-finite values.
Results may differ from the reference program's by a relative error of at most 0.005.
Values may be sent and summed in bfloat16 or wider, within the bound.
No kernel may reach another device: no remote copies, remote signals or barrier semaphores. Data moves between devices by JAX's collectives and lax.ppermute only.
A program may use at most 192 MiB of HBM per device.

```python
import jax
import jax.numpy as jnp

F = 256
BLOCK = 128
RB_DEV = 32
TPB = 32
CAP = 1024
N = 131072
NB = 1024
N_ROWS = 32


def draw_tile_count(key, part):
    key = jax.random.fold_in(key, 7)
    counts = jax.random.randint(key, (N_ROWS,), CAP // 2, CAP + 1)
    chosen = jax.random.randint(jax.random.fold_in(key, 1), (), 0, N_ROWS)
    return counts.at[chosen].set(CAP).astype(jnp.int32)


def touch_ends(drawn, stream_key, least, top_value):
    index_at = [jax.random.randint(jax.random.fold_in(stream_key, axis), (), 0, length) for axis, length in enumerate(drawn.shape)]
    longest = drawn.shape.index(max(drawn.shape))
    beside = index_at[:longest] + [(index_at[longest] + 1) % drawn.shape[longest]] + index_at[longest + 1:]
    return drawn.at[tuple(index_at)].set(least).at[tuple(beside)].set(top_value)


def level_of(rng, shape, shards, least, top_value):
    def one(dim, shards_of):
        steps = jax.random.uniform(jax.random.fold_in(jax.random.fold_in(rng, 6), dim), (shards_of,), jnp.float32, least / len(shards), top_value / len(shards))
        return jnp.repeat(jnp.exp(steps), shape[dim] // shards_of).reshape((-1,) + (1,) * (len(shape) - dim - 1))

    level = one(*shards[0])
    for cut in shards[1:]:
        level = level * one(*cut)
    return level


def noise(rng, shape, deviation, most, pieces=(), kind=jnp.bfloat16):
    gain = level_of(rng, shape, pieces, -0.22, 0.18) if pieces else 1.0
    drawn = jax.random.normal(rng, shape, jnp.float32) * deviation * gain
    return jnp.minimum(jnp.maximum(drawn, -most), most).astype(kind)


def setup_inputs(seed: int = 0) -> dict:
    key_of = jax.random.split(jax.random.key(seed), 8)
    features = noise(key_of[0], (F, N), 1.0, 6.0, ((0, 8), (1, 32)))
    weight = noise(key_of[1], (F, F), F ** -0.5, 0.375)
    adj_tiles = noise(key_of[2], (N_ROWS * CAP, BLOCK, BLOCK), (1.0 / (BLOCK * TPB) ** 0.5), 0.09375, ((0, 32),))
    tile_rows = touch_ends(jax.random.randint(key_of[3], (N_ROWS * CAP,), 0, RB_DEV), jax.random.fold_in(key_of[3], 1), 0, RB_DEV - 1).astype(jnp.int32)
    tile_cols = touch_ends(jax.random.randint(key_of[4], (N_ROWS * CAP,), 0, NB), jax.random.fold_in(key_of[4], 1), 0, NB - 1).astype(jnp.int32)
    tile_count = draw_tile_count(jax.random.fold_in(key_of[7], 71), 0)
    cotangent = noise(key_of[6], (F, N), 1.0, 6.0, ((0, 8), (1, 32)))
    return dict(features=features, weight=weight, adj_tiles=adj_tiles, tile_rows=tile_rows, tile_cols=tile_cols, tile_count=tile_count, cotangent=cotangent)


def reference(features, weight, adj_tiles, tile_rows, tile_cols, tile_count, cotangent):
    width = features.shape[0]
    nodes = features.shape[1]
    side = adj_tiles.shape[1]
    nblocks = nodes // side
    slots = adj_tiles.shape[0] // N_ROWS
    number = jnp.arange(adj_tiles.shape[0], dtype=jnp.int32)
    holder = number // slots
    valid = ((number % slots) < tile_count[holder]).astype(jnp.float32)
    grow = holder * (nblocks // N_ROWS) + tile_rows
    tiles32 = adj_tiles.astype(jnp.float32)
    hidden = jnp.dot(features.T, weight, preferred_element_type=jnp.float32).astype(jnp.bfloat16)
    picked = hidden.reshape(nblocks, side, width)[tile_cols].astype(jnp.float32)
    terms = jnp.einsum('tij,tjf->tif', tiles32, picked) * valid[:, None, None]
    summed = jax.ops.segment_sum(terms, grow, nblocks).reshape(nodes, width)
    aggregated = summed.astype(jnp.bfloat16).T
    grad_rows = cotangent.T.reshape(nblocks, side, width)[grow].astype(jnp.float32)
    reverse = jnp.einsum('tij,tif->tjf', tiles32, grad_rows) * valid[:, None, None]
    dhidden = jax.ops.segment_sum(reverse, tile_cols, nblocks).reshape(nodes, width).astype(jnp.bfloat16)
    grad_features = jnp.dot(dhidden, weight.T, preferred_element_type=jnp.float32).astype(jnp.bfloat16).T
    grad_weight = jnp.dot(features, dhidden, preferred_element_type=jnp.float32)
    return aggregated, grad_features, grad_weight
```

```python
import functools

import jax
import jax.numpy as jnp
from jax import lax
from jax.experimental import pallas as pl
from jax.experimental.pallas import tpu as pltpu
from jax.sharding import Mesh
from jax.sharding import PartitionSpec as P

TB = 128
MIB = 1024 * 1024


def zero(ref):
    @pl.loop(0, ref.shape[0] // 16)
    def _(i):
        ref[pl.ds(i * 16, 16)] = jnp.zeros((16,) + ref.shape[1:], ref.dtype)


def each_tile(count, tb, one):
    base = pl.program_id(0) * tb

    @pl.when(base + tb <= count)
    def _():
        for k in range(tb):
            one(base + k, k)

    @pl.when((base < count) & (base + tb > count))
    def _():
        @pl.loop(0, count - base)
        def _(k):
            one(base + k, k)


def reverse_body(rows_ref, places_ref, count_ref, grads_ref, tiles_ref, *rest, tb):
    outs, total = rest[:-1], rest[-1]

    @pl.when(pl.program_id(0) == 0)
    def _():
        zero(total)

    def one(slot, k):
        total[places_ref[slot]] += jnp.dot(
            grads_ref[rows_ref[slot]], tiles_ref[k], preferred_element_type=jnp.float32
        )

    each_tile(count_ref[0], tb, one)

    @pl.when(pl.program_id(0) == pl.num_programs(0) - 1)
    def _():
        for i, out in enumerate(outs):
            @pl.loop(0, out.shape[0] // 8)
            def _(j):
                out[pl.ds(j * 8, 8)] = total[pl.ds(i * out.shape[0] + j * 8, 8)].astype(out.dtype)


def forward_body(rows_ref, cols_ref, count_ref, panel_ref, tiles_ref, out_ref, total, *, tb):
    @pl.when(pl.program_id(0) == 0)
    def _():
        zero(total)

    def one(slot, k):
        total[rows_ref[slot]] += lax.dot_general(
            panel_ref[cols_ref[slot]], tiles_ref[k], (((1,), (1,)), ((), ())),
            preferred_element_type=jnp.float32,
        )

    each_tile(count_ref[0], tb, one)

    @pl.when(pl.program_id(0) == pl.num_programs(0) - 1)
    def _():
        out_ref[...] = total[...].astype(out_ref.dtype)


def tile_pass(body, rows, cols, count, resident, tiles, total, outs, name):
    slots, side, _ = tiles.shape
    narrow = resident.shape[1]

    def fetch(i, rows_ref, cols_ref, count_ref):
        return (jnp.minimum(i, jnp.maximum((count_ref[0] + TB - 1) // TB - 1, 0)), 0, 0)

    out = [jax.ShapeDtypeStruct((total // outs, narrow, side), jnp.bfloat16)] * outs
    return pl.pallas_call(
        functools.partial(body, tb=TB),
        out_shape=out,
        grid_spec=pltpu.PrefetchScalarGridSpec(
            num_scalar_prefetch=3,
            grid=(slots // TB,),
            in_specs=[
                pl.BlockSpec(memory_space=pltpu.VMEM),
                pl.BlockSpec((TB, side, side), fetch),
            ],
            out_specs=[pl.BlockSpec(memory_space=pltpu.VMEM)] * outs,
            scratch_shapes=[pltpu.VMEM((total, narrow, side), jnp.float32)],
        ),
        compiler_params=pltpu.CompilerParams(vmem_limit_bytes=40 * MIB),
        cost_estimate=pl.CostEstimate(
            flops=16 * slots * narrow * side * side,
            bytes_accessed=2 * slots * side * side + 6 * total * narrow * side,
            transcendentals=0,
        ),
        name=name,
    )(rows, cols, count, resident, tiles)


def exchange(parts, axis):
    return lax.all_to_all(parts, axis, split_axis=0, concat_axis=0, tiled=True)


def total_of_all(term):
    width = term.shape[1]
    n_cols, n_rows = lax.axis_size("cols"), lax.axis_size(("z", "x"))
    per_col = exchange(term, "cols").reshape(n_cols, term.shape[0] // n_cols, width).sum(0)
    per_row = exchange(per_col, ("z", "x")).reshape(n_rows, -1, width).sum(0)
    per_col = exchange(jnp.tile(per_row, (n_rows, 1)), ("z", "x"))
    return exchange(jnp.tile(per_col, (n_cols, 1)), "cols")


def on_device(features, weight, adj_tiles, tile_rows, tile_cols, tile_count, cotangent):
    side = adj_tiles.shape[1]
    narrow, local_nodes = features.shape
    blocks = local_nodes // side
    nz, nx, nc = lax.axis_size("z"), lax.axis_size("x"), lax.axis_size("cols")
    z, x, c = lax.axis_index("z"), lax.axis_index("x"), lax.axis_index("cols")

    def to_blocks(a):
        return jnp.transpose(a.reshape(narrow, blocks, side), (1, 0, 2))

    def from_blocks(a):
        return jnp.transpose(a, (1, 0, 2)).reshape(narrow, local_nodes)

    panel = lax.all_gather(to_blocks(features), ("z", "x"), axis=0, tiled=True)

    grad_full = lax.all_to_all(cotangent, "cols", split_axis=1, concat_axis=0, tiled=True)
    turned = jnp.dot(weight, grad_full, preferred_element_type=jnp.float32).astype(jnp.bfloat16)
    turned = lax.all_to_all(turned, "cols", split_axis=0, concat_axis=1, tiled=True)

    turn = 1 - 2 * (c % 2)
    owner = tile_cols // blocks
    far_x = (turn * (owner % nx - x)) % nx
    far_z = (turn * (owner // nx - z)) % nz
    early = nz // 2
    late_first = (far_z - (early - 1)) % nz
    place = ((late_first // early * nx + far_x) * early + late_first % early) * blocks + tile_cols % blocks
    terms = tile_pass(
        reverse_body, tile_rows, place, tile_count, to_blocks(turned), adj_tiles,
        nz * nx * blocks, 2 * nx, "reverse",
    )

    def ring(a, axis, n, ahead):
        moves = [(i * nc + j, (i + ahead * (1 - 2 * (j % 2))) % n * nc + j) for i in range(n) for j in range(nc)]
        return lax.ppermute(a, (axis, "cols"), moves)

    def add(*terms):
        return sum(t.astype(jnp.float32) for t in terms)

    held = {}
    for part in range(2):
        t0, t1, t2, t3 = terms[part * nx:(part + 1) * nx]
        m2 = ring(t2, "x", nx, 1)
        m3 = ring(t3, "x", nx, -1)
        m1 = ring(add(t1, m2).astype(jnp.bfloat16), "x", nx, 1)
        for i in range(early):
            cut = slice(i * blocks, (i + 1) * blocks)
            held[(part * early + i + early - 1) % nz] = (t0[cut], m1[cut], m3[cut])
    ahead, behind = (), ()
    for step in range(4):
        ahead = (ring(add(*held[4 - step], *ahead).astype(jnp.bfloat16), "z", nz, 1),)
        if step < 3:
            behind = (ring(add(*held[5 + step], *behind).astype(jnp.bfloat16), "z", nz, -1),)
    grad_features = from_blocks(add(*held[0], *ahead, *behind).astype(jnp.bfloat16))

    (mixed,) = tile_pass(
        forward_body, tile_rows, tile_cols, tile_count, panel, adj_tiles, blocks, 1, "forward"
    )
    mixed_full = lax.all_to_all(from_blocks(mixed), "cols", split_axis=1, concat_axis=0, tiled=True)
    aggregated = lax.dot_general(
        weight, mixed_full, (((0,), (0,)), ((), ())), preferred_element_type=jnp.float32
    ).astype(jnp.bfloat16)
    aggregated = lax.all_to_all(aggregated, "cols", split_axis=0, concat_axis=1, tiled=True)
    grad_weight = total_of_all(
        lax.dot_general(
            mixed_full, grad_full, (((1,), (1,)), ((), ())), preferred_element_type=jnp.float32
        )
    )
    return (aggregated, grad_features, grad_weight)


def solution(mesh):
    torus = Mesh(mesh.devices.reshape(8, 4, 8), ("z", "x", "cols"))
    rows = ("z", "x")
    placed = (
        P("cols", rows),
        P(),
        P(rows, None, None),
        P(rows),
        P(rows),
        P(rows),
        P("cols", rows),
    )
    return jax.shard_map(
        on_device,
        mesh=torus,
        in_specs=placed,
        out_specs=(P("cols", rows), P("cols", rows), P()),
        check_vma=False,
    )
```

```python
import functools

import jax
import jax.numpy as jnp
from jax import lax
from jax.experimental import pallas as pl
from jax.experimental.pallas import tpu as pltpu
from jax.sharding import Mesh
from jax.sharding import PartitionSpec as P

TB = 128
STRIP = 16
MIB = 1024 * 1024


def zero(ref):
    @pl.loop(0, ref.shape[0] // 16)
    def _(i):
        ref[pl.ds(i * 16, 16)] = jnp.zeros((16,) + ref.shape[1:], ref.dtype)


def each_tile(count, tb, one):
    base = pl.program_id(0) * tb

    @pl.when(base + tb <= count)
    def _():
        for k in range(tb):
            one(base + k, k, None)

    @pl.when((base < count) & (base + tb > count))
    def _():
        @pl.loop(0, (count - base + STRIP - 1) // STRIP)
        def _(strip):
            for i in range(STRIP):
                k = strip * STRIP + i
                one(base + k, k, base + k < count)


def kept(term, used):
    return term if used is None else jnp.where(used, term, 0.0)


def reverse_body(rows_ref, places_ref, count_ref, grads_ref, tiles_ref, *rest, tb):
    outs, total = rest[:-1], rest[-1]

    @pl.when(pl.program_id(0) == 0)
    def _():
        zero(total)

    def one(slot, k, used):
        term = jnp.dot(grads_ref[rows_ref[slot]], tiles_ref[k], preferred_element_type=jnp.float32)
        total[places_ref[slot]] += kept(term, used)

    each_tile(count_ref[0], tb, one)

    @pl.when(pl.program_id(0) == pl.num_programs(0) - 1)
    def _():
        base = 0
        for out in outs:
            @pl.loop(0, out.shape[0] // 8)
            def _(j):
                out[pl.ds(j * 8, 8)] = total[pl.ds(base + j * 8, 8)].astype(out.dtype)

            base += out.shape[0]


def forward_body(rows_ref, cols_ref, count_ref, panel_ref, tiles_ref, out_ref, total, *, tb):
    @pl.when(pl.program_id(0) == 0)
    def _():
        zero(total)

    def one(slot, k, used):
        term = lax.dot_general(
            panel_ref[cols_ref[slot]], tiles_ref[k], (((1,), (1,)), ((), ())),
            preferred_element_type=jnp.float32,
        )
        total[rows_ref[slot]] += kept(term, used)

    each_tile(count_ref[0], tb, one)

    @pl.when(pl.program_id(0) == pl.num_programs(0) - 1)
    def _():
        out_ref[...] = total[...].astype(out_ref.dtype)


def tile_pass(body, rows, places, count, resident, tiles, outs, name):
    slots, side, _ = tiles.shape
    narrow = resident.shape[1]

    def fetch(i, rows_ref, places_ref, count_ref):
        return (jnp.minimum(i, jnp.maximum((count_ref[0] + TB - 1) // TB - 1, 0)), 0, 0)

    total = sum(outs)
    return pl.pallas_call(
        functools.partial(body, tb=TB),
        out_shape=[jax.ShapeDtypeStruct((n, narrow, side), jnp.bfloat16) for n in outs],
        grid_spec=pltpu.PrefetchScalarGridSpec(
            num_scalar_prefetch=3,
            grid=(slots // TB,),
            in_specs=[pl.BlockSpec(memory_space=pltpu.VMEM), pl.BlockSpec((TB, side, side), fetch)],
            out_specs=[pl.BlockSpec(memory_space=pltpu.VMEM)] * len(outs),
            scratch_shapes=[pltpu.VMEM((total, narrow, side), jnp.float32)],
        ),
        compiler_params=pltpu.CompilerParams(vmem_limit_bytes=40 * MIB),
        cost_estimate=pl.CostEstimate(
            flops=16 * slots * narrow * side * side,
            bytes_accessed=2 * slots * side * side + 2 * (total + resident.shape[0]) * narrow * side,
            transcendentals=0,
        ),
        name=name,
    )(rows, places, count, resident, tiles)


def exchange(parts, axis):
    return lax.all_to_all(parts, axis, split_axis=0, concat_axis=0, tiled=True)


def together(*arrays):
    return lax.optimization_barrier(arrays)


def to_all(a, axis):
    return exchange(jnp.tile(a, (lax.axis_size(axis),) + (1,) * (a.ndim - 1)), axis)


def on_device(features, weight, adj_tiles, tile_rows, tile_cols, tile_count, cotangent):
    side = adj_tiles.shape[1]
    narrow, local_nodes = features.shape
    blocks = local_nodes // side
    nz, nx, nc = lax.axis_size("z"), lax.axis_size("x"), lax.axis_size("cols")
    z, x, c = lax.axis_index("z"), lax.axis_index("x"), lax.axis_index("cols")

    def to_blocks(a):
        return jnp.transpose(a.reshape(narrow, blocks, side), (1, 0, 2))

    def from_blocks(a):
        return jnp.transpose(a, (1, 0, 2)).reshape(narrow, local_nodes)

    turn = 1 - 2 * (c % 2)
    owner = tile_cols // blocks
    far_x = (turn * (owner % nx - x)) % nx
    far_z = (turn * (owner // nx - z)) % nz
    x_first = blocks // 2
    z_first = blocks - x_first
    inner = tile_cols % blocks
    place = jnp.where(
        inner < x_first,
        (far_x * nz + far_z) * x_first + inner,
        nx * nz * x_first + (far_z * nx + far_x) * z_first + inner - x_first,
    )
    def ring(a, axis, n, ahead):
        moves = [(i * nc + j, (i + ahead * (1 - 2 * (j % 2))) % n * nc + j) for i in range(n) for j in range(nc)]
        return lax.ppermute(a, (axis, "cols"), moves)

    panel = lax.all_gather(to_blocks(features), ("z", "x"), axis=0, tiled=True)

    per_col = weight.reshape(nc, narrow, nc, narrow)
    split = (nc, blocks // nc, narrow, side)
    whole = (blocks, narrow, side)
    turned = exchange(to_blocks(cotangent), "cols").reshape(split)
    turned = jnp.einsum("dgcf,cbfn->dbgn", per_col, turned, preferred_element_type=jnp.float32)
    turned = exchange(turned.astype(jnp.bfloat16).reshape(whole), "cols")
    turned, spread = together(turned, cotangent)
    grad_full = to_all(spread, "cols")
    terms = tile_pass(
        reverse_body, tile_rows, place, tile_count, turned, adj_tiles,
        (nz * x_first,) * nx + (nx * z_first,) * nz, "reverse",
    )

    def add(*terms):
        return sum(t.astype(jnp.float32) for t in terms)

    def narrowed(*terms):
        return add(*terms).astype(jnp.bfloat16)

    *terms, grad_full = together(*terms, grad_full)
    by_x, by_z = terms[:nx], terms[nx:]
    m2 = ring(by_x[2], "x", nx, 1)
    m3 = ring(by_x[3], "x", nx, -1)
    ahead, behind = ring(by_z[4], "z", nz, 1), ring(by_z[5], "z", nz, -1)
    ahead, behind = together(narrowed(by_z[3], ahead), narrowed(by_z[6], behind))
    ahead, behind = ring(ahead, "z", nz, 1), ring(behind, "z", nz, -1)
    m2, m3, ahead, behind = together(m2, m3, ahead, behind)

    m1 = ring(narrowed(by_x[1], m2), "x", nx, 1)
    ahead = ring(narrowed(by_z[2], ahead), "z", nz, 1)
    behind = ring(narrowed(by_z[7], behind), "z", nz, -1)
    m1, ahead, behind, count = together(m1, ahead, behind, tile_count)

    def held(*far):
        cut = slice(far[0] * x_first, (far[-1] + 1) * x_first)
        return by_x[0][cut], m1[cut], m3[cut]

    n34 = ring(narrowed(*held(3, 4)), "z", nz, 2)
    n56 = ring(narrowed(*held(5, 6)), "z", nz, -2)
    ahead = ring(narrowed(by_z[1], ahead), "z", nz, 1)
    (mixed,) = tile_pass(
        forward_body, tile_rows, tile_cols, count, panel, adj_tiles, (blocks,), "forward"
    )
    n34, n56, ahead, mixed = together(n34, n56, ahead, mixed)

    mixed_full = exchange(mixed, "cols").reshape(split)
    term = lax.dot_general(
        from_blocks(mixed), grad_full, (((1,), (1,)), ((), ())), preferred_element_type=jnp.float32
    )
    shares = to_all(term.astype(jnp.bfloat16)[None], ("z", "x"))
    n2 = ring(narrowed(*held(2), n34[x_first:]), "z", nz, 2)
    n1 = ring(narrowed(*held(1), n34[:x_first]), "z", nz, 1)
    n7 = ring(narrowed(*held(7), n56[:x_first]), "z", nz, -1)
    line = add(by_z[0], ahead, behind).reshape(nx, z_first, narrow, side)
    late = add(line[0], *(ring(narrowed(line[i]), "x", nx, (0, 1, 2, -1)[i]) for i in (1, 2, 3)))

    aggregated = jnp.einsum(
        "cfdg,cbfn->dbgn", per_col, mixed_full, preferred_element_type=jnp.float32
    ).astype(jnp.bfloat16)
    whole_term = shares.astype(jnp.float32).sum(0).reshape(narrow, -1, side).transpose(1, 0, 2)
    top = whole_term.astype(jnp.bfloat16)
    rest = (whole_term - top.astype(jnp.float32)).astype(jnp.bfloat16)
    for_all = jnp.broadcast_to(jnp.concatenate([top, rest], 0), (nc, 2 * top.shape[0], narrow, side))
    back = exchange(jnp.concatenate([aggregated, for_all], 1), "cols")
    n_own, n_top = split[1], top.shape[0]
    aggregated = from_blocks(back[:, :n_own].reshape(whole))
    top, rest = back[:, n_own:n_own + n_top], back[:, n_own + n_top:]
    grad_weight = add(top, rest).transpose(0, 2, 1, 3).reshape(nc * narrow, -1)

    soon = add(*held(0), n56[x_first:], n2, n1, n7)
    grad_features = from_blocks(jnp.concatenate([soon, late], 0).astype(jnp.bfloat16))
    return (aggregated, grad_features, grad_weight)


def solution(mesh):
    torus = Mesh(mesh.devices.reshape(8, 4, 8), ("z", "x", "cols"))
    rows = ("z", "x")
    placed = (
        P("cols", rows),
        P(),
        P(rows, None, None),
        P(rows),
        P(rows),
        P(rows),
        P("cols", rows),
    )
    return jax.shard_map(
        on_device,
        mesh=torus,
        in_specs=placed,
        out_specs=(P("cols", rows), P("cols", rows), P()),
        check_vma=False,
    )
```

```python
import functools

import jax
import jax.numpy as jnp
from jax import lax
from jax.experimental import pallas as pl
from jax.experimental.pallas import tpu as pltpu
from jax.sharding import Mesh
from jax.sharding import PartitionSpec as P

TB = 128
STRIP = 16
MIB = 1024 * 1024


def zero(ref):
    @pl.loop(0, ref.shape[0] // 16)
    def _(i):
        ref[pl.ds(i * 16, 16)] = jnp.zeros((16,) + ref.shape[1:], ref.dtype)


def each_tile(count, tb, one):
    base = pl.program_id(0) * tb

    @pl.when(base + tb <= count)
    def _():
        for k in range(tb):
            one(base + k, k, None)

    @pl.when((base < count) & (base + tb > count))
    def _():
        @pl.loop(0, (count - base + STRIP - 1) // STRIP)
        def _(strip):
            for i in range(STRIP):
                k = strip * STRIP + i
                one(base + k, k, base + k < count)


def kept(term, used):
    return term if used is None else jnp.where(used, term, 0.0)


def reverse_body(rows_ref, places_ref, count_ref, grads_ref, tiles_ref, *rest, tb):
    outs, total = rest[:-1], rest[-1]

    @pl.when(pl.program_id(0) == 0)
    def _():
        zero(total)

    def one(slot, k, used):
        term = jnp.dot(grads_ref[rows_ref[slot]], tiles_ref[k], preferred_element_type=jnp.float32)
        total[places_ref[slot]] += kept(term, used)

    each_tile(count_ref[0], tb, one)

    @pl.when(pl.program_id(0) == pl.num_programs(0) - 1)
    def _():
        base = 0
        for out in outs:
            @pl.loop(0, out.shape[0] // 8)
            def _(j):
                out[pl.ds(j * 8, 8)] = total[pl.ds(base + j * 8, 8)].astype(out.dtype)

            base += out.shape[0]


def forward_body(rows_ref, places_ref, count_ref, *rest, tb, pieces):
    parts, (tiles_ref, out_ref, total, panel, sems) = rest[:pieces], rest[pieces:]

    @pl.when(pl.program_id(0) == 0)
    def _():
        base, copies = 0, []
        for i, part in enumerate(parts):
            copies.append(pltpu.make_async_copy(part, panel.at[pl.ds(base, part.shape[0])], sems.at[i]))
            base += part.shape[0]
        for copy in copies:
            copy.start()
        zero(total)
        for copy in copies:
            copy.wait()

    def one(slot, k, used):
        term = lax.dot_general(
            panel[places_ref[slot]], tiles_ref[k], (((1,), (1,)), ((), ())),
            preferred_element_type=jnp.float32,
        )
        total[rows_ref[slot]] += kept(term, used)

    each_tile(count_ref[0], tb, one)

    @pl.when(pl.program_id(0) == pl.num_programs(0) - 1)
    def _():
        out_ref[...] = total[...].astype(out_ref.dtype)


def tile_pass(body, rows, places, count, resident, resident_spec, tiles, outs, scratch, room, name):
    slots, side, _ = tiles.shape
    narrow = resident[0].shape[1]

    def fetch(i, rows_ref, places_ref, count_ref):
        return (jnp.minimum(i, jnp.maximum((count_ref[0] + TB - 1) // TB - 1, 0)), 0, 0)

    total = sum(outs)
    moved = 2 * (slots * side * side + (total + sum(r.shape[0] for r in resident)) * narrow * side)
    return pl.pallas_call(
        body,
        out_shape=[jax.ShapeDtypeStruct((n, narrow, side), jnp.bfloat16) for n in outs],
        grid_spec=pltpu.PrefetchScalarGridSpec(
            num_scalar_prefetch=3,
            grid=(slots // TB,),
            in_specs=[resident_spec] * len(resident) + [pl.BlockSpec((TB, side, side), fetch)],
            out_specs=[pl.BlockSpec(memory_space=pltpu.VMEM)] * len(outs),
            scratch_shapes=[pltpu.VMEM((total, narrow, side), jnp.float32)] + scratch,
        ),
        compiler_params=pltpu.CompilerParams(vmem_limit_bytes=room * MIB),
        cost_estimate=pl.CostEstimate(
            flops=16 * slots * narrow * side * side, bytes_accessed=moved, transcendentals=0
        ),
        name=name,
    )(rows, places, count, *resident, tiles)


def exchange(parts, axis):
    return lax.all_to_all(parts, axis, split_axis=0, concat_axis=0, tiled=True)


def together(*arrays):
    return lax.optimization_barrier(arrays)


def to_all(a, axis):
    return exchange(jnp.tile(a, (lax.axis_size(axis),) + (1,) * (a.ndim - 1)), axis)


def on_device(features, weight, adj_tiles, tile_rows, tile_cols, tile_count, cotangent):
    side = adj_tiles.shape[1]
    narrow, local_nodes = features.shape
    blocks = local_nodes // side
    nz, nx, nc = lax.axis_size("z"), lax.axis_size("x"), lax.axis_size("cols")
    z, x, c = lax.axis_index("z"), lax.axis_index("x"), lax.axis_index("cols")

    def to_blocks(a):
        return jnp.transpose(a.reshape(narrow, blocks, side), (1, 0, 2))

    def from_blocks(a):
        return jnp.transpose(a, (1, 0, 2)).reshape(narrow, local_nodes)

    def ring(a, axis, n, ahead):
        moves = [(i * nc + j, (i + ahead * (1 - 2 * (j % 2))) % n * nc + j) for i in range(n) for j in range(nc)]
        return lax.ppermute(a, (axis, "cols"), moves)

    def add(*terms):
        return sum(t.astype(jnp.float32) for t in terms)

    def narrowed(*terms):
        return add(*terms).astype(jnp.bfloat16)

    turn = 1 - 2 * (c % 2)
    owner = tile_cols // blocks
    far_x = (turn * (owner % nx - x)) % nx
    far_z = (turn * (owner // nx - z)) % nz
    inner = tile_cols % blocks
    most = blocks * 5 // 8
    few = blocks - most
    source = jnp.where(
        inner < most, owner * most + inner, nz * nx * most + (far_z * nx + far_x) * few + inner - most
    )
    x_first = blocks // 2
    z_first = blocks - x_first
    place = jnp.where(
        inner < x_first,
        (far_x * nz + far_z) * x_first + inner,
        nx * nz * x_first + (far_z * nx + far_x) * z_first + inner - x_first,
    )

    mine = to_blocks(features)
    gathered = lax.all_gather(mine[:most], ("z", "x"), axis=0, tiled=True)
    s1, s2, s3 = (ring(mine[most:], "x", nx, step) for step in (1, 2, -1))

    per_col = weight.reshape(nc, narrow, nc, narrow)
    split = (nc, blocks // nc, narrow, side)
    whole = (blocks, narrow, side)
    turned = exchange(to_blocks(cotangent), "cols").reshape(split)
    s1, s2, s3, turned = together(s1, s2, s3, turned)
    start = jnp.concatenate([mine[most:], s3, s2, s1], 0)
    before, after = [ring(start, "z", nz, 1)], [start, ring(start, "z", nz, -1)]
    turned = jnp.einsum("dgcf,cbfn->dbgn", per_col, turned, preferred_element_type=jnp.float32)
    turned = exchange(turned.astype(jnp.bfloat16).reshape(whole), "cols")
    turned, before[0], after[1] = together(turned, before[0], after[1])
    before.append(ring(before[0], "z", nz, 1))
    after.append(ring(after[1], "z", nz, -1))
    turned, before[1], after[2] = together(turned, before[1], after[2])
    before.append(ring(before[1], "z", nz, 1))
    after.append(ring(after[2], "z", nz, -1))
    in_vmem = pl.BlockSpec(memory_space=pltpu.VMEM)
    terms = tile_pass(
        functools.partial(reverse_body, tb=TB), tile_rows, place, tile_count, [turned], in_vmem, adj_tiles,
        (nz * x_first,) * nx + (nx * z_first,) * nz, [], 40, "reverse",
    )
    *terms, spread, before[2], after[3] = together(*terms, cotangent, before[2], after[3])
    grad_full = to_all(spread, "cols")

    by_x, by_z = terms[:nx], terms[nx:]
    before.append(ring(before[2], "z", nz, 1))
    m2 = ring(by_x[2], "x", nx, 1)
    m3 = ring(by_x[3], "x", nx, -1)
    ahead, behind = ring(by_z[4], "z", nz, 1), ring(by_z[5], "z", nz, -1)
    ahead, behind, before[3], count = together(
        narrowed(by_z[3], ahead), narrowed(by_z[6], behind), before[3], tile_count
    )
    ahead, behind = ring(ahead, "z", nz, 1), ring(behind, "z", nz, -1)
    panel = [gathered, *after, *before[::-1]]
    (mixed,) = tile_pass(
        functools.partial(forward_body, tb=TB, pieces=len(panel)), tile_rows, source, count, panel,
        pl.BlockSpec(memory_space=pl.ANY), adj_tiles, (blocks,),
        [
            pltpu.VMEM((nz * nx * blocks, narrow, side), jnp.bfloat16),
            pltpu.SemaphoreType.DMA((len(panel),)),
        ],
        56, "forward",
    )
    m2, m3, ahead, behind, grad_full, mixed = together(m2, m3, ahead, behind, grad_full, mixed)

    m1 = ring(narrowed(by_x[1], m2), "x", nx, 1)
    ahead = ring(narrowed(by_z[2], ahead), "z", nz, 1)
    behind = ring(narrowed(by_z[7], behind), "z", nz, -1)
    mixed_full = exchange(mixed, "cols").reshape(split)
    term = lax.dot_general(
        from_blocks(mixed), grad_full, (((1,), (1,)), ((), ())), preferred_element_type=jnp.float32
    ).astype(jnp.bfloat16)
    m1, ahead, behind, mixed_full, term = together(m1, ahead, behind, mixed_full, term)

    def held(*far):
        cut = slice(far[0] * x_first, (far[-1] + 1) * x_first)
        return by_x[0][cut], m1[cut], m3[cut]

    n34 = ring(narrowed(*held(3, 4)), "z", nz, 2)
    n56 = ring(narrowed(*held(5, 6)), "z", nz, -2)
    ahead = ring(narrowed(by_z[1], ahead), "z", nz, 1)
    n34, n56, term, mixed_full = together(n34, n56, term, mixed_full)
    shares = to_all(term[None], ("z", "x"))
    aggregated = jnp.einsum(
        "cfdg,cbfn->dbgn", per_col, mixed_full, preferred_element_type=jnp.float32
    ).astype(jnp.bfloat16)
    n2 = ring(narrowed(*held(2), n34[x_first:]), "z", nz, 2)
    n1 = ring(narrowed(*held(1), n34[:x_first]), "z", nz, 1)
    n7 = ring(narrowed(*held(7), n56[:x_first]), "z", nz, -1)
    line = add(by_z[0], ahead, behind).reshape(nx, z_first, narrow, side)
    late = add(line[0], *(ring(narrowed(line[i]), "x", nx, (0, 1, 2, -1)[i]) for i in (1, 2, 3)))
    whole_term = shares.astype(jnp.float32).sum(0).reshape(narrow, -1, side).transpose(1, 0, 2)
    top = whole_term.astype(jnp.bfloat16)
    rest = (whole_term - top.astype(jnp.float32)).astype(jnp.bfloat16)
    for_all = jnp.broadcast_to(jnp.concatenate([top, rest], 0), (nc, 2 * top.shape[0], narrow, side))
    back = exchange(jnp.concatenate([aggregated, for_all], 1), "cols")
    n_own, n_top = split[1], top.shape[0]
    aggregated = from_blocks(back[:, :n_own].reshape(whole))
    top, rest = back[:, n_own:n_own + n_top], back[:, n_own + n_top:]
    grad_weight = add(top, rest).transpose(0, 2, 1, 3).reshape(nc * narrow, -1)

    soon = add(*held(0), n56[x_first:], n2, n1, n7)
    grad_features = from_blocks(jnp.concatenate([soon, late], 0).astype(jnp.bfloat16))
    return (aggregated, grad_features, grad_weight)


def solution(mesh):
    torus = Mesh(mesh.devices.reshape(8, 4, 8), ("z", "x", "cols"))
    rows = ("z", "x")
    placed = (
        P("cols", rows),
        P(),
        P(rows, None, None),
        P(rows),
        P(rows),
        P(rows),
        P("cols", rows),
    )
    return jax.shard_map(
        on_device,
        mesh=torus,
        in_specs=placed,
        out_specs=(P("cols", rows), P("cols", rows), P()),
        check_vma=False,
    )
```

```python
import functools

import jax
import jax.numpy as jnp
from jax import lax
from jax.experimental import pallas as pl
from jax.experimental.pallas import tpu as pltpu
from jax.sharding import Mesh
from jax.sharding import PartitionSpec as P

TB = 128
STRIP = 16
MIB = 1024 * 1024


def zero(ref):
    @pl.loop(0, ref.shape[0] // 16)
    def _(i):
        ref[pl.ds(i * 16, 16)] = jnp.zeros((16,) + ref.shape[1:], ref.dtype)


def each_tile(count, tb, one):
    base = pl.program_id(0) * tb

    @pl.when(base + tb <= count)
    def _():
        for k in range(tb):
            one(base + k, k, None)

    @pl.when((base < count) & (base + tb > count))
    def _():
        @pl.loop(0, (count - base + STRIP - 1) // STRIP)
        def _(strip):
            for i in range(STRIP):
                k = strip * STRIP + i
                one(base + k, k, base + k < count)


def kept(term, used):
    return term if used is None else jnp.where(used, term, 0.0)


def reverse_body(rows_ref, places_ref, count_ref, grads_ref, tiles_ref, *rest, tb):
    outs, total = rest[:-1], rest[-1]

    @pl.when(pl.program_id(0) == 0)
    def _():
        zero(total)

    def one(slot, k, used):
        term = jnp.dot(grads_ref[rows_ref[slot]], tiles_ref[k], preferred_element_type=jnp.float32)
        total[places_ref[slot]] += kept(term, used)

    each_tile(count_ref[0], tb, one)

    @pl.when(pl.program_id(0) == pl.num_programs(0) - 1)
    def _():
        base = 0
        for out in outs:
            @pl.loop(0, out.shape[0] // 8)
            def _(j):
                out[pl.ds(j * 8, 8)] = total[pl.ds(base + j * 8, 8)].astype(out.dtype)

            base += out.shape[0]


def forward_body(rows_ref, places_ref, count_ref, *rest, tb, pieces):
    parts, (tiles_ref, out_ref, total, panel, sems) = rest[:pieces], rest[pieces:]

    @pl.when(pl.program_id(0) == 0)
    def _():
        base, copies = 0, []
        for i, part in enumerate(parts):
            copies.append(pltpu.make_async_copy(part, panel.at[pl.ds(base, part.shape[0])], sems.at[i]))
            base += part.shape[0]
        for copy in copies:
            copy.start()
        zero(total)
        for copy in copies:
            copy.wait()

    def one(slot, k, used):
        term = lax.dot_general(
            panel[places_ref[slot]], tiles_ref[k], (((1,), (1,)), ((), ())),
            preferred_element_type=jnp.float32,
        )
        total[rows_ref[slot]] += kept(term, used)

    each_tile(count_ref[0], tb, one)

    @pl.when(pl.program_id(0) == pl.num_programs(0) - 1)
    def _():
        out_ref[...] = total[...].astype(out_ref.dtype)


def tile_pass(body, rows, places, count, resident, resident_spec, tiles, outs, scratch, room, name):
    slots, side, _ = tiles.shape
    narrow = resident[0].shape[1]

    def fetch(i, rows_ref, places_ref, count_ref):
        return (jnp.minimum(i, jnp.maximum((count_ref[0] + TB - 1) // TB - 1, 0)), 0, 0)

    total = sum(outs)
    moved = 2 * (slots * side * side + (total + sum(r.shape[0] for r in resident)) * narrow * side)
    return pl.pallas_call(
        body,
        out_shape=[jax.ShapeDtypeStruct((n, narrow, side), jnp.bfloat16) for n in outs],
        grid_spec=pltpu.PrefetchScalarGridSpec(
            num_scalar_prefetch=3,
            grid=(slots // TB,),
            in_specs=[resident_spec] * len(resident) + [pl.BlockSpec((TB, side, side), fetch)],
            out_specs=[pl.BlockSpec(memory_space=pltpu.VMEM)] * len(outs),
            scratch_shapes=[pltpu.VMEM((total, narrow, side), jnp.float32)] + scratch,
        ),
        compiler_params=pltpu.CompilerParams(vmem_limit_bytes=room * MIB),
        cost_estimate=pl.CostEstimate(
            flops=16 * slots * narrow * side * side, bytes_accessed=moved, transcendentals=0
        ),
        name=name,
    )(rows, places, count, *resident, tiles)


def exchange(parts, axis):
    return lax.all_to_all(parts, axis, split_axis=0, concat_axis=0, tiled=True)


def together(*arrays):
    return lax.optimization_barrier(arrays)


def to_all(a, axis):
    return exchange(jnp.tile(a, (lax.axis_size(axis),) + (1,) * (a.ndim - 1)), axis)


def on_device(features, weight, adj_tiles, tile_rows, tile_cols, tile_count, cotangent):
    side = adj_tiles.shape[1]
    narrow, local_nodes = features.shape
    blocks = local_nodes // side
    nz, nx, nc = lax.axis_size("z"), lax.axis_size("x"), lax.axis_size("cols")
    z, x, c = lax.axis_index("z"), lax.axis_index("x"), lax.axis_index("cols")

    def to_blocks(a):
        return jnp.transpose(a.reshape(narrow, blocks, side), (1, 0, 2))

    def from_blocks(a):
        return jnp.transpose(a, (1, 0, 2)).reshape(narrow, local_nodes)

    def ring(a, axis, n, ahead):
        moves = [(i * nc + j, (i + ahead * (1 - 2 * (j % 2))) % n * nc + j) for i in range(n) for j in range(nc)]
        return lax.ppermute(a, (axis, "cols"), moves)

    def add(*terms):
        return sum(t.astype(jnp.float32) for t in terms)

    def narrowed(*terms):
        return add(*terms).astype(jnp.bfloat16)

    turn = 1 - 2 * (c % 2)
    owner = tile_cols // blocks
    far_x = (turn * (owner % nx - x)) % nx
    far_z = (turn * (owner // nx - z)) % nz
    inner = tile_cols % blocks
    most = blocks * 5 // 8
    few = blocks - most
    source = jnp.where(
        inner < most, owner * most + inner, nz * nx * most + (far_z * nx + far_x) * few + inner - most
    )
    x_first = blocks // 2
    z_first = blocks - x_first
    place = jnp.where(
        inner < x_first,
        (far_x * nz + far_z) * x_first + inner,
        nx * nz * x_first + (far_z * nx + far_x) * z_first + inner - x_first,
    )

    mine = to_blocks(features)
    gathered = lax.all_gather(mine[:most], ("z", "x"), axis=0, tiled=True)
    s1, s2, s3 = (ring(mine[most:], "x", nx, step) for step in (1, 2, -1))

    per_col = weight.reshape(nc, narrow, nc, narrow)
    split = (nc, blocks // nc, narrow, side)
    whole = (blocks, narrow, side)
    turned = exchange(to_blocks(cotangent), "cols").reshape(split)
    s1, s2, s3, turned = together(s1, s2, s3, turned)
    start = jnp.concatenate([mine[most:], s3, s2, s1], 0)
    before, after = [ring(start, "z", nz, 1)], [start, ring(start, "z", nz, -1)]
    turned = jnp.einsum("dgcf,cbfn->dbgn", per_col, turned, preferred_element_type=jnp.float32)
    turned = exchange(turned.astype(jnp.bfloat16).reshape(whole), "cols")
    turned, before[0], after[1] = together(turned, before[0], after[1])
    before.append(ring(before[0], "z", nz, 1))
    after.append(ring(after[1], "z", nz, -1))
    turned, before[1], after[2] = together(turned, before[1], after[2])
    before.append(ring(before[1], "z", nz, 1))
    after.append(ring(after[2], "z", nz, -1))
    in_vmem = pl.BlockSpec(memory_space=pltpu.VMEM)
    terms = tile_pass(
        functools.partial(reverse_body, tb=TB), tile_rows, place, tile_count, [turned], in_vmem, adj_tiles,
        (nz * x_first,) * nx + (nx * z_first,) * nz, [], 40, "reverse",
    )
    *terms, spread, before[2], after[3] = together(*terms, cotangent, before[2], after[3])
    grad_full = to_all(spread, "cols")

    by_x, by_z = terms[:nx], terms[nx:]
    before.append(ring(before[2], "z", nz, 1))
    m2 = ring(by_x[2], "x", nx, 1)
    m3 = ring(by_x[3], "x", nx, -1)
    ahead, behind = ring(by_z[4], "z", nz, 1), ring(by_z[5], "z", nz, -1)
    ahead, behind, before[3], count = together(
        narrowed(by_z[3], ahead), narrowed(by_z[6], behind), before[3], tile_count
    )
    ahead, behind = ring(ahead, "z", nz, 1), ring(behind, "z", nz, -1)
    panel = [gathered, *after, *before[::-1]]
    (mixed,) = tile_pass(
        functools.partial(forward_body, tb=TB, pieces=len(panel)), tile_rows, source, count, panel,
        pl.BlockSpec(memory_space=pl.ANY), adj_tiles, (blocks,),
        [
            pltpu.VMEM((nz * nx * blocks, narrow, side), jnp.bfloat16),
            pltpu.SemaphoreType.DMA((len(panel),)),
        ],
        56, "forward",
    )
    m2, m3, ahead, behind, grad_full, mixed = together(m2, m3, ahead, behind, grad_full, mixed)

    m1 = ring(narrowed(by_x[1], m2), "x", nx, 1)
    ahead = ring(narrowed(by_z[2], ahead), "z", nz, 1)
    behind = ring(narrowed(by_z[7], behind), "z", nz, -1)
    mixed_full = exchange(mixed, "cols").reshape(split)
    term = lax.dot_general(
        from_blocks(mixed), grad_full, (((1,), (1,)), ((), ())), preferred_element_type=jnp.float32
    ).astype(jnp.bfloat16)
    m1, ahead, behind, mixed_full, term = together(m1, ahead, behind, mixed_full, term)

    def held(*far):
        cut = slice(far[0] * x_first, (far[-1] + 1) * x_first)
        return by_x[0][cut], m1[cut], m3[cut]

    n34 = ring(narrowed(*held(3, 4)), "z", nz, 2)
    n56 = ring(narrowed(*held(5, 6)), "z", nz, -2)
    ahead = ring(narrowed(by_z[1], ahead), "z", nz, 1)
    ahead, term = together(ahead, term)
    shares = to_all(term[None], ("z", "x"))
    n34, n56, mixed_full = together(n34, n56, mixed_full)
    aggregated = jnp.einsum(
        "cfdg,cbfn->dbgn", per_col, mixed_full, preferred_element_type=jnp.float32
    ).astype(jnp.bfloat16)
    n2 = ring(narrowed(*held(2), n34[x_first:]), "z", nz, 2)
    n1 = ring(narrowed(*held(1), n34[:x_first]), "z", nz, 1)
    n7 = ring(narrowed(*held(7), n56[:x_first]), "z", nz, -1)
    line = add(by_z[0], ahead, behind).reshape(nx, z_first, narrow, side)
    late = add(line[0], *(ring(narrowed(line[i]), "x", nx, (0, 1, 2, -1)[i]) for i in (1, 2, 3)))
    whole_term = shares.astype(jnp.float32).sum(0).reshape(narrow, -1, side).transpose(1, 0, 2)
    top = whole_term.astype(jnp.bfloat16)
    rest = (whole_term - top.astype(jnp.float32)).astype(jnp.bfloat16)
    for_all = jnp.broadcast_to(jnp.concatenate([top, rest], 0), (nc, 2 * top.shape[0], narrow, side))
    back = exchange(jnp.concatenate([aggregated, for_all], 1), "cols")
    n_own, n_top = split[1], top.shape[0]
    aggregated = from_blocks(back[:, :n_own].reshape(whole))
    top, rest = back[:, n_own:n_own + n_top], back[:, n_own + n_top:]
    grad_weight = add(top, rest).transpose(0, 2, 1, 3).reshape(nc * narrow, -1)

    soon = add(*held(0), n56[x_first:], n2, n1, n7)
    grad_features = from_blocks(jnp.concatenate([soon, late], 0).astype(jnp.bfloat16))
    return (aggregated, grad_features, grad_weight)


def solution(mesh):
    torus = Mesh(mesh.devices.reshape(8, 4, 8), ("z", "x", "cols"))
    rows = ("z", "x")
    placed = (
        P("cols", rows),
        P(),
        P(rows, None, None),
        P(rows),
        P(rows),
        P(rows),
        P("cols", rows),
    )
    return jax.shard_map(
        on_device,
        mesh=torus,
        in_specs=placed,
        out_specs=(P("cols", rows), P("cols", rows), P()),
        check_vma=False,
    )
```

```python
import functools

import jax
import jax.numpy as jnp
from jax import lax
from jax.experimental import pallas as pl
from jax.experimental.pallas import tpu as pltpu
from jax.sharding import Mesh
from jax.sharding import PartitionSpec as P

TB = 128
STRIP = 16
MIB = 1024 * 1024


def zero(ref):
    @pl.loop(0, ref.shape[0] // 16)
    def _(i):
        ref[pl.ds(i * 16, 16)] = jnp.zeros((16,) + ref.shape[1:], ref.dtype)


def each_tile(count, tb, one):
    base = pl.program_id(0) * tb

    @pl.when(base + tb <= count)
    def _():
        for k in range(tb):
            one(base + k, k, None)

    @pl.when((base < count) & (base + tb > count))
    def _():
        @pl.loop(0, (count - base + STRIP - 1) // STRIP)
        def _(strip):
            for i in range(STRIP):
                k = strip * STRIP + i
                one(base + k, k, base + k < count)


def kept(term, used):
    return term if used is None else jnp.where(used, term, 0.0)


def reverse_body(rows_ref, places_ref, count_ref, grads_ref, tiles_ref, *rest, tb):
    outs, total = rest[:-1], rest[-1]

    @pl.when(pl.program_id(0) == 0)
    def _():
        zero(total)

    def one(slot, k, used):
        term = jnp.dot(grads_ref[rows_ref[slot]], tiles_ref[k], preferred_element_type=jnp.float32)
        total[places_ref[slot]] += kept(term, used)

    each_tile(count_ref[0], tb, one)

    @pl.when(pl.program_id(0) == pl.num_programs(0) - 1)
    def _():
        base = 0
        for out in outs:
            @pl.loop(0, out.shape[0] // 8)
            def _(j):
                out[pl.ds(j * 8, 8)] = total[pl.ds(base + j * 8, 8)].astype(out.dtype)

            base += out.shape[0]


def forward_body(rows_ref, places_ref, count_ref, *rest, tb, pieces):
    parts, (tiles_ref, out_ref, total, panel, sems) = rest[:pieces], rest[pieces:]

    @pl.when(pl.program_id(0) == 0)
    def _():
        base, copies = 0, []
        for i, part in enumerate(parts):
            copies.append(pltpu.make_async_copy(part, panel.at[pl.ds(base, part.shape[0])], sems.at[i]))
            base += part.shape[0]
        for copy in copies:
            copy.start()
        zero(total)
        for copy in copies:
            copy.wait()

    def one(slot, k, used):
        term = lax.dot_general(
            panel[places_ref[slot]], tiles_ref[k], (((1,), (1,)), ((), ())),
            preferred_element_type=jnp.float32,
        )
        total[rows_ref[slot]] += kept(term, used)

    each_tile(count_ref[0], tb, one)

    @pl.when(pl.program_id(0) == pl.num_programs(0) - 1)
    def _():
        out_ref[...] = total[...].astype(out_ref.dtype)


def tile_pass(body, rows, places, count, resident, resident_spec, tiles, outs, scratch, room, name):
    slots, side, _ = tiles.shape
    narrow = resident[0].shape[1]

    def fetch(i, rows_ref, places_ref, count_ref):
        return (jnp.minimum(i, jnp.maximum((count_ref[0] + TB - 1) // TB - 1, 0)), 0, 0)

    total = sum(outs)
    moved = 2 * (slots * side * side + (total + sum(r.shape[0] for r in resident)) * narrow * side)
    return pl.pallas_call(
        body,
        out_shape=[jax.ShapeDtypeStruct((n, narrow, side), jnp.bfloat16) for n in outs],
        grid_spec=pltpu.PrefetchScalarGridSpec(
            num_scalar_prefetch=3,
            grid=(slots // TB,),
            in_specs=[resident_spec] * len(resident) + [pl.BlockSpec((TB, side, side), fetch)],
            out_specs=[pl.BlockSpec(memory_space=pltpu.VMEM)] * len(outs),
            scratch_shapes=[pltpu.VMEM((total, narrow, side), jnp.float32)] + scratch,
        ),
        compiler_params=pltpu.CompilerParams(vmem_limit_bytes=room * MIB),
        cost_estimate=pl.CostEstimate(
            flops=16 * slots * narrow * side * side, bytes_accessed=moved, transcendentals=0
        ),
        name=name,
    )(rows, places, count, *resident, tiles)


def exchange(parts, axis):
    return lax.all_to_all(parts, axis, split_axis=0, concat_axis=0, tiled=True)


def together(*arrays):
    return lax.optimization_barrier(arrays)


def to_all(a, axis):
    return exchange(jnp.tile(a, (lax.axis_size(axis),) + (1,) * (a.ndim - 1)), axis)


def on_device(features, weight, adj_tiles, tile_rows, tile_cols, tile_count, cotangent):
    side = adj_tiles.shape[1]
    narrow, local_nodes = features.shape
    blocks = local_nodes // side
    nz, nx, nc = lax.axis_size("z"), lax.axis_size("x"), lax.axis_size("cols")
    z, x, c = lax.axis_index("z"), lax.axis_index("x"), lax.axis_index("cols")

    def to_blocks(a):
        return jnp.transpose(a.reshape(narrow, blocks, side), (1, 0, 2))

    def from_blocks(a):
        return jnp.transpose(a, (1, 0, 2)).reshape(narrow, local_nodes)

    def ring(a, axis, n, ahead):
        moves = [(i * nc + j, (i + ahead * (1 - 2 * (j % 2))) % n * nc + j) for i in range(n) for j in range(nc)]
        return lax.ppermute(a, (axis, "cols"), moves)

    def add(*terms):
        return sum(t.astype(jnp.float32) for t in terms)

    def narrowed(*terms):
        return add(*terms).astype(jnp.bfloat16)

    turn = 1 - 2 * (c % 2)
    owner = tile_cols // blocks
    far_x = (turn * (owner % nx - x)) % nx
    far_z = (turn * (owner // nx - z)) % nz
    inner = tile_cols % blocks
    most = blocks * 5 // 8
    few = blocks - most
    source = jnp.where(
        inner < most, owner * most + inner, nz * nx * most + (far_z * nx + far_x) * few + inner - most
    )
    x_first = blocks // 2
    z_first = blocks - x_first
    place = jnp.where(
        inner < x_first,
        (far_x * nz + far_z) * x_first + inner,
        nx * nz * x_first + (far_z * nx + far_x) * z_first + inner - x_first,
    )

    mine = to_blocks(features)
    gathered = lax.all_gather(mine[:most], ("z", "x"), axis=0, tiled=True)
    s1, s2, s3 = (ring(mine[most:], "x", nx, step) for step in (1, 2, -1))

    per_col = weight.reshape(nc, narrow, nc, narrow)
    split = (nc, blocks // nc, narrow, side)
    whole = (blocks, narrow, side)
    turned = exchange(to_blocks(cotangent), "cols").reshape(split)
    s1, s2, s3, turned = together(s1, s2, s3, turned)
    start = jnp.concatenate([mine[most:], s3, s2, s1], 0)
    before, after = [ring(start, "z", nz, 1)], [start, ring(start, "z", nz, -1)]
    turned = jnp.einsum("dgcf,cbfn->dbgn", per_col, turned, preferred_element_type=jnp.float32)
    turned = exchange(turned.astype(jnp.bfloat16).reshape(whole), "cols")
    turned, before[0], after[1] = together(turned, before[0], after[1])
    before.append(ring(before[0], "z", nz, 1))
    after.append(ring(after[1], "z", nz, -1))
    turned, before[1], after[2] = together(turned, before[1], after[2])
    before.append(ring(before[1], "z", nz, 1))
    after.append(ring(after[2], "z", nz, -1))
    in_vmem = pl.BlockSpec(memory_space=pltpu.VMEM)
    terms = tile_pass(
        functools.partial(reverse_body, tb=TB), tile_rows, place, tile_count, [turned], in_vmem, adj_tiles,
        (nz * x_first,) * nx + (nx * z_first,) * nz, [], 40, "reverse",
    )
    *terms, spread, before[2], after[3] = together(*terms, cotangent, before[2], after[3])
    grad_full = to_all(spread, "cols")

    by_x, by_z = terms[:nx], terms[nx:]
    before.append(ring(before[2], "z", nz, 1))
    m2 = ring(by_x[2], "x", nx, 1)
    m3 = ring(by_x[3], "x", nx, -1)
    ahead, behind = ring(by_z[4], "z", nz, 1), ring(by_z[5], "z", nz, -1)
    ahead, behind, before[3], count = together(
        narrowed(by_z[3], ahead), narrowed(by_z[6], behind), before[3], tile_count
    )
    ahead, behind = ring(ahead, "z", nz, 1), ring(behind, "z", nz, -1)
    panel = [gathered, *after, *before[::-1]]
    (mixed,) = tile_pass(
        functools.partial(forward_body, tb=TB, pieces=len(panel)), tile_rows, source, count, panel,
        pl.BlockSpec(memory_space=pl.ANY), adj_tiles, (blocks,),
        [
            pltpu.VMEM((nz * nx * blocks, narrow, side), jnp.bfloat16),
            pltpu.SemaphoreType.DMA((len(panel),)),
        ],
        56, "forward",
    )
    m2, m3, ahead, behind, grad_full, mixed = together(m2, m3, ahead, behind, grad_full, mixed)

    m1 = ring(narrowed(by_x[1], m2), "x", nx, 1)
    ahead = ring(narrowed(by_z[2], ahead), "z", nz, 1)
    behind = ring(narrowed(by_z[7], behind), "z", nz, -1)
    mixed_full = exchange(mixed, "cols").reshape(split)
    term = lax.dot_general(
        from_blocks(mixed), grad_full, (((1,), (1,)), ((), ())), preferred_element_type=jnp.float32
    ).astype(jnp.bfloat16)
    m1, ahead, behind, mixed_full, term = together(m1, ahead, behind, mixed_full, term)

    def held(*far):
        cut = slice(far[0] * x_first, (far[-1] + 1) * x_first)
        return by_x[0][cut], m1[cut], m3[cut]

    n34 = ring(narrowed(*held(3, 4)), "z", nz, 2)
    n56 = ring(narrowed(*held(5, 6)), "z", nz, -2)
    ahead = ring(narrowed(by_z[1], ahead), "z", nz, 1)
    shares = to_all(term[None], ("z", "x"))
    n34, n56, shares, mixed_full = together(n34, n56, shares, mixed_full)
    aggregated = jnp.einsum(
        "cfdg,cbfn->dbgn", per_col, mixed_full, preferred_element_type=jnp.float32
    ).astype(jnp.bfloat16)
    n2 = ring(narrowed(*held(2), n34[x_first:]), "z", nz, 2)
    n1 = ring(narrowed(*held(1), n34[:x_first]), "z", nz, 1)
    n7 = ring(narrowed(*held(7), n56[:x_first]), "z", nz, -1)
    line = add(by_z[0], ahead, behind).reshape(nx, z_first, narrow, side)
    late = add(line[0], *(ring(narrowed(line[i]), "x", nx, (0, 1, 2, -1)[i]) for i in (1, 2, 3)))
    whole_term = shares.astype(jnp.float32).sum(0).reshape(narrow, -1, side).transpose(1, 0, 2)
    top = whole_term.astype(jnp.bfloat16)
    rest = (whole_term - top.astype(jnp.float32)).astype(jnp.bfloat16)
    for_all = jnp.broadcast_to(jnp.concatenate([top, rest], 0), (nc, 2 * top.shape[0], narrow, side))
    back = exchange(jnp.concatenate([aggregated, for_all], 1), "cols")
    n_own, n_top = split[1], top.shape[0]
    aggregated = from_blocks(back[:, :n_own].reshape(whole))
    top, rest = back[:, n_own:n_own + n_top], back[:, n_own + n_top:]
    grad_weight = add(top, rest).transpose(0, 2, 1, 3).reshape(nc * narrow, -1)

    soon = add(*held(0), n56[x_first:], n2, n1, n7)
    grad_features = from_blocks(jnp.concatenate([soon, late], 0).astype(jnp.bfloat16))
    return (aggregated, grad_features, grad_weight)


def solution(mesh):
    torus = Mesh(mesh.devices.reshape(8, 4, 8), ("z", "x", "cols"))
    rows = ("z", "x")
    placed = (
        P("cols", rows),
        P(),
        P(rows, None, None),
        P(rows),
        P(rows),
        P(rows),
        P("cols", rows),
    )
    return jax.shard_map(
        on_device,
        mesh=torus,
        in_specs=placed,
        out_specs=(P("cols", rows), P("cols", rows), P()),
        check_vma=False,
    )
```

```python
import functools

import jax
import jax.numpy as jnp
from jax import lax
from jax.experimental import pallas as pl
from jax.experimental.pallas import tpu as pltpu
from jax.sharding import Mesh
from jax.sharding import PartitionSpec as P

TB = 128
STRIP = 16
MIB = 1024 * 1024


def zero(ref):
    @pl.loop(0, ref.shape[0] // 16)
    def _(i):
        ref[pl.ds(i * 16, 16)] = jnp.zeros((16,) + ref.shape[1:], ref.dtype)


def each_tile(count, tb, one):
    base = pl.program_id(0) * tb

    @pl.when(base + tb <= count)
    def _():
        for k in range(tb):
            one(base + k, k, None)

    @pl.when((base < count) & (base + tb > count))
    def _():
        @pl.loop(0, (count - base + STRIP - 1) // STRIP)
        def _(strip):
            for i in range(STRIP):
                k = strip * STRIP + i
                one(base + k, k, base + k < count)


def kept(term, used):
    return term if used is None else jnp.where(used, term, 0.0)


def reverse_body(rows_ref, places_ref, count_ref, grads_ref, tiles_ref, *rest, tb):
    outs, total = rest[:-1], rest[-1]

    @pl.when(pl.program_id(0) == 0)
    def _():
        zero(total)

    def one(slot, k, used):
        term = jnp.dot(grads_ref[rows_ref[slot]], tiles_ref[k], preferred_element_type=jnp.float32)
        total[places_ref[slot]] += kept(term, used)

    each_tile(count_ref[0], tb, one)

    @pl.when(pl.program_id(0) == pl.num_programs(0) - 1)
    def _():
        base = 0
        for out in outs:
            @pl.loop(0, out.shape[0] // 8)
            def _(j):
                out[pl.ds(j * 8, 8)] = total[pl.ds(base + j * 8, 8)].astype(out.dtype)

            base += out.shape[0]


def forward_body(rows_ref, places_ref, count_ref, *rest, tb, pieces):
    parts, (tiles_ref, out_ref, total, panel, sems) = rest[:pieces], rest[pieces:]

    @pl.when(pl.program_id(0) == 0)
    def _():
        base, copies = 0, []
        for i, part in enumerate(parts):
            copies.append(pltpu.make_async_copy(part, panel.at[pl.ds(base, part.shape[0])], sems.at[i]))
            base += part.shape[0]
        for copy in copies:
            copy.start()
        zero(total)
        for copy in copies:
            copy.wait()

    def one(slot, k, used):
        term = lax.dot_general(
            panel[places_ref[slot]], tiles_ref[k], (((1,), (1,)), ((), ())),
            preferred_element_type=jnp.float32,
        )
        total[rows_ref[slot]] += kept(term, used)

    each_tile(count_ref[0], tb, one)

    @pl.when(pl.program_id(0) == pl.num_programs(0) - 1)
    def _():
        out_ref[...] = total[...].astype(out_ref.dtype)


def tile_pass(body, rows, places, count, resident, resident_spec, tiles, outs, scratch, room, name):
    slots, side, _ = tiles.shape
    narrow = resident[0].shape[1]

    def fetch(i, rows_ref, places_ref, count_ref):
        return (jnp.minimum(i, jnp.maximum((count_ref[0] + TB - 1) // TB - 1, 0)), 0, 0)

    total = sum(outs)
    moved = 2 * (slots * side * side + (total + sum(r.shape[0] for r in resident)) * narrow * side)
    return pl.pallas_call(
        body,
        out_shape=[jax.ShapeDtypeStruct((n, narrow, side), jnp.bfloat16) for n in outs],
        grid_spec=pltpu.PrefetchScalarGridSpec(
            num_scalar_prefetch=3,
            grid=(slots // TB,),
            in_specs=[resident_spec] * len(resident) + [pl.BlockSpec((TB, side, side), fetch)],
            out_specs=[pl.BlockSpec(memory_space=pltpu.VMEM)] * len(outs),
            scratch_shapes=[pltpu.VMEM((total, narrow, side), jnp.float32)] + scratch,
        ),
        compiler_params=pltpu.CompilerParams(vmem_limit_bytes=room * MIB),
        cost_estimate=pl.CostEstimate(
            flops=16 * slots * narrow * side * side, bytes_accessed=moved, transcendentals=0
        ),
        name=name,
    )(rows, places, count, *resident, tiles)


def exchange(parts, axis):
    return lax.all_to_all(parts, axis, split_axis=0, concat_axis=0, tiled=True)


def together(*arrays):
    return lax.optimization_barrier(arrays)


def to_all(a, axis):
    return exchange(jnp.tile(a, (lax.axis_size(axis),) + (1,) * (a.ndim - 1)), axis)


def on_device(features, weight, adj_tiles, tile_rows, tile_cols, tile_count, cotangent):
    side = adj_tiles.shape[1]
    narrow, local_nodes = features.shape
    blocks = local_nodes // side
    nz, nx, nc = lax.axis_size("z"), lax.axis_size("x"), lax.axis_size("cols")
    z, x, c = lax.axis_index("z"), lax.axis_index("x"), lax.axis_index("cols")

    def to_blocks(a):
        return jnp.transpose(a.reshape(narrow, blocks, side), (1, 0, 2))

    def from_blocks(a):
        return jnp.transpose(a, (1, 0, 2)).reshape(narrow, local_nodes)

    def ring(a, axis, n, ahead):
        moves = [(i * nc + j, (i + ahead * (1 - 2 * (j % 2))) % n * nc + j) for i in range(n) for j in range(nc)]
        return lax.ppermute(a, (axis, "cols"), moves)

    def add(*terms):
        return sum(t.astype(jnp.float32) for t in terms)

    def narrowed(*terms):
        return add(*terms).astype(jnp.bfloat16)

    turn = 1 - 2 * (c % 2)
    owner = tile_cols // blocks
    far_x = (turn * (owner % nx - x)) % nx
    far_z = (turn * (owner // nx - z)) % nz
    inner = tile_cols % blocks
    most = blocks * 3 // 4
    few = blocks - most
    source = jnp.where(
        inner < most, owner * most + inner, nz * nx * most + (far_z * nx + far_x) * few + inner - most
    )
    x_first = blocks // 2
    z_first = blocks - x_first
    place = jnp.where(
        inner < x_first,
        (far_x * nz + far_z) * x_first + inner,
        nx * nz * x_first + (far_z * nx + far_x) * z_first + inner - x_first,
    )

    mine = to_blocks(features)
    gathered = lax.all_gather(mine[:most], ("z", "x"), axis=0, tiled=True)
    s1, s2, s3 = (ring(mine[most:], "x", nx, step) for step in (1, 2, -1))

    per_col = weight.reshape(nc, narrow, nc, narrow)
    split = (nc, blocks // nc, narrow, side)
    whole = (blocks, narrow, side)
    turned = exchange(to_blocks(cotangent), "cols").reshape(split)
    s1, s2, s3, turned = together(s1, s2, s3, turned)
    start = jnp.concatenate([mine[most:], s3, s2, s1], 0)
    before, after = [ring(start, "z", nz, 1)], [start, ring(start, "z", nz, -1)]
    turned = jnp.einsum("dgcf,cbfn->dbgn", per_col, turned, preferred_element_type=jnp.float32)
    turned = exchange(turned.astype(jnp.bfloat16).reshape(whole), "cols")
    turned, before[0], after[1] = together(turned, before[0], after[1])
    before.append(ring(before[0], "z", nz, 1))
    after.append(ring(after[1], "z", nz, -1))
    turned, before[1], after[2] = together(turned, before[1], after[2])
    before.append(ring(before[1], "z", nz, 1))
    after.append(ring(after[2], "z", nz, -1))
    in_vmem = pl.BlockSpec(memory_space=pltpu.VMEM)
    terms = tile_pass(
        functools.partial(reverse_body, tb=TB), tile_rows, place, tile_count, [turned], in_vmem, adj_tiles,
        (nz * x_first,) * nx + (nx * z_first,) * nz, [], 40, "reverse",
    )
    *terms, spread, before[2], after[3] = together(*terms, cotangent, before[2], after[3])
    grad_full = to_all(spread, "cols")

    by_x, by_z = terms[:nx], terms[nx:]
    before.append(ring(before[2], "z", nz, 1))
    m2 = ring(by_x[2], "x", nx, 1)
    m3 = ring(by_x[3], "x", nx, -1)
    ahead, behind = ring(by_z[4], "z", nz, 1), ring(by_z[5], "z", nz, -1)
    ahead, behind, before[3], count = together(
        narrowed(by_z[3], ahead), narrowed(by_z[6], behind), before[3], tile_count
    )
    ahead, behind = ring(ahead, "z", nz, 1), ring(behind, "z", nz, -1)
    panel = [gathered, *after, *before[::-1]]
    (mixed,) = tile_pass(
        functools.partial(forward_body, tb=TB, pieces=len(panel)), tile_rows, source, count, panel,
        pl.BlockSpec(memory_space=pl.ANY), adj_tiles, (blocks,),
        [
            pltpu.VMEM((nz * nx * blocks, narrow, side), jnp.bfloat16),
            pltpu.SemaphoreType.DMA((len(panel),)),
        ],
        56, "forward",
    )
    m2, m3, ahead, behind, grad_full, mixed = together(m2, m3, ahead, behind, grad_full, mixed)

    m1 = ring(narrowed(by_x[1], m2), "x", nx, 1)
    ahead = ring(narrowed(by_z[2], ahead), "z", nz, 1)
    behind = ring(narrowed(by_z[7], behind), "z", nz, -1)
    mixed_full = exchange(mixed, "cols").reshape(split)
    term = lax.dot_general(
        from_blocks(mixed), grad_full, (((1,), (1,)), ((), ())), preferred_element_type=jnp.float32
    ).astype(jnp.bfloat16)
    m1, ahead, behind, mixed_full, term = together(m1, ahead, behind, mixed_full, term)

    def held(*far):
        cut = slice(far[0] * x_first, (far[-1] + 1) * x_first)
        return by_x[0][cut], m1[cut], m3[cut]

    n34 = ring(narrowed(*held(3, 4)), "z", nz, 2)
    n56 = ring(narrowed(*held(5, 6)), "z", nz, -2)
    ahead = ring(narrowed(by_z[1], ahead), "z", nz, 1)
    shares = to_all(term[None], ("z", "x"))
    n34, n56, shares, mixed_full = together(n34, n56, shares, mixed_full)
    aggregated = jnp.einsum(
        "cfdg,cbfn->dbgn", per_col, mixed_full, preferred_element_type=jnp.float32
    ).astype(jnp.bfloat16)
    n2 = ring(narrowed(*held(2), n34[x_first:]), "z", nz, 2)
    n1 = ring(narrowed(*held(1), n34[:x_first]), "z", nz, 1)
    n7 = ring(narrowed(*held(7), n56[:x_first]), "z", nz, -1)
    line = add(by_z[0], ahead, behind).reshape(nx, z_first, narrow, side)
    late = add(line[0], *(ring(narrowed(line[i]), "x", nx, (0, 1, 2, -1)[i]) for i in (1, 2, 3)))
    whole_term = shares.astype(jnp.float32).sum(0).reshape(narrow, -1, side).transpose(1, 0, 2)
    top = whole_term.astype(jnp.bfloat16)
    rest = (whole_term - top.astype(jnp.float32)).astype(jnp.bfloat16)
    for_all = jnp.broadcast_to(jnp.concatenate([top, rest], 0), (nc, 2 * top.shape[0], narrow, side))
    back = exchange(jnp.concatenate([aggregated, for_all], 1), "cols")
    n_own, n_top = split[1], top.shape[0]
    aggregated = from_blocks(back[:, :n_own].reshape(whole))
    top, rest = back[:, n_own:n_own + n_top], back[:, n_own + n_top:]
    grad_weight = add(top, rest).transpose(0, 2, 1, 3).reshape(nc * narrow, -1)

    soon = add(*held(0), n56[x_first:], n2, n1, n7)
    grad_features = from_blocks(jnp.concatenate([soon, late], 0).astype(jnp.bfloat16))
    return (aggregated, grad_features, grad_weight)


def solution(mesh):
    torus = Mesh(mesh.devices.reshape(8, 4, 8), ("z", "x", "cols"))
    rows = ("z", "x")
    placed = (
        P("cols", rows),
        P(),
        P(rows, None, None),
        P(rows),
        P(rows),
        P(rows),
        P("cols", rows),
    )
    return jax.shard_map(
        on_device,
        mesh=torus,
        in_specs=placed,
        out_specs=(P("cols", rows), P("cols", rows), P()),
        check_vma=False,
    )
```
